32 devices in a mesh: grp: 2 (over y), row: 4 (over z), head: 2 (over x), sub: 2 (over core).
Axes of the slice: x: 2, y: 2, z: 4, core: 2. Of those that a mesh axis runs over, the one named last changes fastest.
Arguments:
- queries: bfloat16 [4, 96, 32, 1024], P('head', ('grp', 'row')), parts along dimension 1, may hold values from -6 to 6
- key_side: bfloat16 [4, 96, 32, 1024], P('head', ('grp', 'row'), None, 'sub'), parts along dimension 1, may hold values from -6 to 6
- value_side: bfloat16 [4, 96, 32, 1024], P('head', ('grp', 'row'), None, 'sub'), parts along dimension 1, may hold values from -6 to 6
- attn_out: bfloat16 [4, 96, 32, 1024], P('head', ('grp', 'row')), parts along dimension 1, may hold values from -1.796875 to 1.796875
- out_grad: bfloat16 [4, 96, 32, 1024], P('head', ('grp', 'row')), parts along dimension 1, may hold values from -24 to 24
- log_norm: float32 [4, 96, 1024], P('head', ('grp', 'row')), parts along dimension 1, may hold values from 7 to 9
- pair_bias: bfloat16 [8, 1024, 1024], P(('grp', 'head'), 'row', 'sub'), parts along dimension 0, may hold values from -6 to 6
- chain_ids: int32 [2048], P('grp'), parts along dimension 0, may hold values from 0 to 7, as said below
- pair_table: int32 [16, 8], P('grp'), parts along dimension 0, may hold values from 0 to 1, as said below
Outputs:
- query_grad: bfloat16 [4, 96, 32, 1024], P('head', ('grp', 'row'), None, 'sub'), parts along dimension 1
- key_grad: bfloat16 [4, 96, 32, 1024], P('head', ('grp', 'row'), None, 'sub'), parts along dimension 1
- value_grad: bfloat16 [4, 96, 32, 1024], P('head', ('grp', 'row'), None, 'sub'), parts along dimension 1
- bias_grad: float32 [8, 1024, 1024], P(('grp', 'head'), 'row', 'sub'), parts along dimension 0
The draws below stay inside these ranges and needn't reach their ends.
There are 2 independent parts, one for each index of `grp`. The reference program is written for one: setup_inputs(seed, part) draws one part's arguments, and reference() takes and returns one part's arrays. A program takes and returns all parts, laid end to end along the dimension named above; each array names one. Nothing has to cross between parts.
Inputs may be any that keep to these rules, and one draw needn't show every extreme that they name: `chain_ids`: chains are contiguous runs of residues, numbered in order from 0; each of the 8 chains holds at least one residue. `pair_table`: entries are 0 or 1 and the diagonal is 1.
All inputs are finite; a program needn't handle non-finite values.
Results may differ from the reference program's by a relative error of at most 0.0059.
Values may be sent and summed in bfloat16 or wider, within the bound.
A program may use at most 128 MiB of HBM per device.

```python
import jax
import jax.numpy as jnp
from jax import lax

H = 4
HD = 32
L = 1024
NC = 8
ROWS = 48


def draw_chain_ids(key, part):
    key = jax.random.fold_in(key, 11)
    cuts = jax.random.permutation(key, L - 1)[:NC - 1].astype(jnp.int32) + 1
    positions = jnp.arange(L, dtype=jnp.int32)
    return jnp.sum((positions[:, None] >= cuts[None, :]).astype(jnp.int32), axis=1).astype(jnp.int32)


def draw_pair_table(key, part):
    key = jax.random.fold_in(key, 23)
    random_bits = jax.random.randint(key, (NC, NC), 0, 2).astype(jnp.int32)
    labels = jnp.arange(NC, dtype=jnp.int32)
    diagonal = (labels[:, None] == labels[None, :]).astype(jnp.int32)
    return jnp.maximum(random_bits, diagonal).astype(jnp.int32)


def steps_of(stream_key, shape, pieces, low, high):
    gain = 1.0
    for axis_at, blocks in pieces:
        draws = jax.random.uniform(jax.random.fold_in(jax.random.fold_in(stream_key, 6), axis_at), (blocks,), jnp.float32, low / len(pieces), high / len(pieces))
        gain = gain * jnp.repeat(jnp.exp(draws), shape[axis_at] // blocks).reshape((-1,) + (1,) * (len(shape) - 1 - axis_at))
    return gain


def noise(stream_key, shape, scale, bound, cuts=(), kind=jnp.bfloat16):
    drawn = scale * jax.random.normal(stream_key, shape, jnp.float32)
    if cuts:
        drawn = drawn * steps_of(stream_key, shape, cuts, -0.22, 0.18)
    return jnp.clip(drawn, -bound, bound).astype(kind)


def setup_inputs(seed: int = 0, part: int = 0) -> dict:
    seeds = jax.random.split(jax.random.key(seed), 10)
    part_keys = jax.random.split(jax.random.fold_in(seeds[9], part), 10)
    return {
        "queries": noise(part_keys[0], (H, ROWS, HD, L), 1.0, 6.0, ((0, 2), (1, 4))),
        "key_side": noise(part_keys[1], (H, ROWS, HD, L), 1.0, 6.0, ((0, 2), (1, 4), (3, 2))),
        "value_side": noise(part_keys[2], (H, ROWS, HD, L), 1.0, 6.0, ((0, 2), (1, 4), (3, 2))),
        "attn_out": noise(part_keys[3], (H, ROWS, HD, L), 0.3, 1.796875, ((0, 2), (1, 4))),
        "out_grad": noise(part_keys[4], (H, ROWS, HD, L), 4.0, 24.0, ((0, 2), (1, 4))),
        "log_norm": jnp.clip(7.0 + 2.0 * jax.random.uniform(part_keys[5], (H, ROWS, L), jnp.float32) ** steps_of(part_keys[5], (H, ROWS, L), ((0, 2), (1, 4)), -0.2, 0.2), 7.0, 9.0),
        "pair_bias": noise(part_keys[6], (H, L, L), 1.0, 6.0, ((0, 2), (1, 4), (2, 2))),
        "chain_ids": draw_chain_ids(jax.random.fold_in(jax.random.fold_in(seeds[9], part), 71), part),
        "pair_table": draw_pair_table(jax.random.fold_in(jax.random.fold_in(seeds[9], part), 71), part),
    }


def row_grads(row_query, row_key, row_value, row_out, row_grad, row_norm, bias, allowed):
    factor = HD ** -0.5
    scores = factor * jnp.dot(row_query.T, row_key, preferred_element_type=jnp.float32) + bias.astype(jnp.float32)
    attn_prob = jnp.where(allowed[None, :], jnp.exp(scores - row_norm[:, None]), jnp.zeros_like(scores))
    prob_low = attn_prob.astype(jnp.bfloat16)
    value_part = jnp.dot(row_grad, prob_low, preferred_element_type=jnp.float32)
    prob_grad = jnp.dot(row_grad.T, row_value, preferred_element_type=jnp.float32)
    row_delta = jnp.sum(row_grad.astype(jnp.float32) * row_out.astype(jnp.float32), axis=0)
    score_grad = attn_prob * (prob_grad - row_delta[:, None])
    score_low = score_grad.astype(jnp.bfloat16)
    query_part = factor * jnp.dot(row_key, score_low.T, preferred_element_type=jnp.float32)
    key_part = factor * jnp.dot(row_query, score_low, preferred_element_type=jnp.float32)
    return (query_part.astype(jnp.bfloat16), key_part.astype(jnp.bfloat16),
            value_part.astype(jnp.bfloat16), score_grad)


def reference(queries, key_side, value_side, attn_out, out_grad, log_norm, pair_bias, chain_ids, pair_table):
    slab_chain = chain_ids[:ROWS]
    allowed_rows = pair_table[slab_chain][:, chain_ids] == 1

    def head_grads(head_args):
        head_query, head_key, head_value, head_out, head_grad, head_norm, head_bias = head_args

        def step(running, row_args):
            row_query, row_key, row_value, row_out, row_grad, row_norm, allowed = row_args
            query_part, key_part, value_part, score_grad = row_grads(
                row_query, row_key, row_value, row_out, row_grad, row_norm, head_bias, allowed)
            return running + score_grad, (query_part, key_part, value_part)

        running, parts = lax.scan(step, jnp.zeros((L, L), jnp.float32),
                                  (head_query, head_key, head_value, head_out, head_grad, head_norm, allowed_rows))
        return parts[0], parts[1], parts[2], running

    query_grad, key_grad, value_grad, bias_grad = lax.map(
        head_grads, (queries, key_side, value_side, attn_out, out_grad, log_norm, pair_bias))
    return query_grad, key_grad, value_grad, bias_grad
```

```python
import functools
import math

import jax
import jax.numpy as jnp
from jax import lax
from jax.experimental import pallas as pl
from jax.experimental.pallas import tpu as pltpu
from jax.sharding import PartitionSpec as P

F32 = jnp.float32
BF16 = jnp.bfloat16
LOG2E = math.log2(math.e)
MASKED = -16384.0


def three_parts(value):
    high = value.astype(BF16).astype(F32)
    rest = value - high
    mid = rest.astype(BF16).astype(F32)
    return high, mid, rest - mid


def prepare_row(h, i, key_first, row_first, refs):
    k_ref, v_ref, o_ref, do_ref, n_ref, ids_ref, chain_ref, table_ref, aug_ref, rhs_ref = refs
    head_dim, length = o_ref.shape[2], o_ref.shape[3]
    keys = k_ref.shape[3]
    delta = jnp.sum(do_ref[h, i].astype(F32) * o_ref[h, i].astype(F32), axis=0, keepdims=True)
    n1, n2, n3 = three_parts(n_ref[h, pl.ds(i, 1), :] * (-LOG2E))
    d1, d2, d3 = three_parts(-delta)
    line = lax.broadcasted_iota(jnp.int32, (head_dim, length), 0)
    aug = jnp.where(line == 3, 1.0, 0.0)
    for at, part in ((0, n1), (1, n2), (2, n3), (4, d1), (5, d2), (6, d3)):
        aug = jnp.where(line == at, part, aug)
    aug_ref[h, i] = aug.astype(BF16)
    key_chain = chain_ref[:, pl.ds(key_first, keys)]
    row_chain = ids_ref[0, row_first + i]
    seen = jnp.zeros((1, keys), jnp.int32)
    for label in range(table_ref.shape[1]):
        seen = jnp.where(key_chain == label, table_ref[row_chain, label], seen)
    shut = jnp.where(seen == 1, 0.0, MASKED)
    scaled = k_ref[h, i].astype(F32) * (head_dim ** -0.5 * LOG2E)
    high = scaled.astype(BF16)
    low = (scaled - high.astype(F32)).astype(BF16)
    line = lax.broadcasted_iota(jnp.int32, (head_dim, keys), 0)
    score_side = jnp.where(line < 3, 1.0, jnp.where(line == 3, shut, 0.0))
    prob_side = jnp.where((line >= 4) & (line < 7), 1.0, 0.0)
    none = jnp.zeros((head_dim, keys), BF16)
    rhs_ref[h, i, :, :keys] = jnp.concatenate([high, low, none, score_side.astype(BF16)], axis=0)
    rhs_ref[h, i, :, keys:] = jnp.concatenate(
        [none, none, v_ref[h, i], prob_side.astype(BF16)], axis=0
    )


def row_step(h, i, columns, refs):
    q_ref, k_ref, do_ref, aug_ref, rhs_ref, bias_ref, acc_ref, dq_ref, dk_ref, dv_ref = refs
    keys = k_ref.shape[3]
    chunk = min(256, keys)
    query = q_ref[h, i, :, columns]
    grad = do_ref[h, i, :, columns]
    left = jnp.concatenate([query, query, grad, aug_ref[h, i, :, columns]], axis=0).T
    dq = None
    for first in range(0, keys, chunk):
        part = pl.ds(first, chunk)
        scores = jnp.dot(left, rhs_ref[h, i, :, part], preferred_element_type=F32)
        prob_grad = jnp.dot(
            left, rhs_ref[h, i, :, pl.ds(keys + first, chunk)], preferred_element_type=F32
        )
        prob = jnp.exp2(scores + bias_ref[:, part])
        score_grad = prob * prob_grad
        acc_ref[:, part] += score_grad
        low = score_grad.astype(BF16)
        dv_ref[i, :, part] += jnp.dot(grad, prob.astype(BF16), preferred_element_type=F32)
        dk_ref[i, :, part] += jnp.dot(query, low, preferred_element_type=F32)
        share = lax.dot_general(
            k_ref[h, i, :, part], low, (((1,), (1,)), ((), ())), preferred_element_type=F32
        )
        dq = share if dq is None else dq + share
    return dq


def local_kernel(
    ids_ref, table_ref, chain_ref, q_ref, k_ref, v_ref, o_ref, do_ref, n_ref, b_ref,
    dq_ref, dk_ref, dv_ref, db_ref, aug_ref, rhs_ref, bias_ref, dk_acc, dv_acc,
):
    heads, rows, head_dim, length = q_ref.shape
    keys = k_ref.shape[3]
    tile = bias_ref.shape[0]
    factor = head_dim ** -0.5
    key_first = pl.multiple_of(lax.axis_index("sub") * keys, keys)
    row_first = lax.axis_index("row") * rows
    prep = (k_ref, v_ref, o_ref, do_ref, n_ref, ids_ref, chain_ref, table_ref, aug_ref, rhs_ref)

    for h in range(heads):
        @pl.loop(0, rows)
        def _(i):
            prepare_row(h, i, key_first, row_first, prep)

    for h in range(heads):
        dk_acc[...] = jnp.zeros_like(dk_acc)
        dv_acc[...] = jnp.zeros_like(dv_acc)

        @pl.loop(0, length // tile)
        def _(block):
            columns = pl.ds(pl.multiple_of(block * tile, tile), tile)
            bias_ref[...] = b_ref[h, columns, :].astype(F32) * LOG2E
            acc_ref = db_ref.at[h, columns, :]
            acc_ref[...] = jnp.zeros_like(acc_ref)
            refs = (
                q_ref, k_ref, do_ref, aug_ref, rhs_ref, bias_ref, acc_ref, dq_ref, dk_acc, dv_acc
            )

            def body(i, carry):
                dq_ref[h, i, :, columns] = factor * row_step(h, i, columns, refs)
                return carry

            lax.fori_loop(0, rows, body, 0, unroll=2 if rows % 2 == 0 else 1)

        dk_ref[h] = (factor * dk_acc[...]).astype(BF16)
        dv_ref[h] = dv_acc[...].astype(BF16)


def per_device(
    queries, key_side, value_side, attn_out, out_grad, log_norm, pair_bias, chain_ids, pair_table
):
    heads, rows, head_dim, length = queries.shape
    keys = key_side.shape[3]
    tile = min(256, length)
    bias_all = lax.all_gather(pair_bias, "row", axis=1, tiled=True)
    vmem = pl.BlockSpec(memory_space=pltpu.VMEM)
    smem = pl.BlockSpec(memory_space=pltpu.SMEM)
    ids = chain_ids.reshape(1, length)
    share, key_grad, value_grad, running = pl.pallas_call(
        local_kernel,
        out_shape=(
            jax.ShapeDtypeStruct((heads, rows, head_dim, length), F32),
            jax.ShapeDtypeStruct((heads, rows, head_dim, keys), BF16),
            jax.ShapeDtypeStruct((heads, rows, head_dim, keys), BF16),
            jax.ShapeDtypeStruct((heads, length, keys), F32),
        ),
        in_specs=[smem, smem] + [vmem] * 8,
        out_specs=(vmem,) * 4,
        scratch_shapes=[
            pltpu.VMEM((heads, rows, head_dim, length), BF16),
            pltpu.VMEM((heads, rows, 4 * head_dim, 2 * keys), BF16),
            pltpu.VMEM((tile, keys), F32),
            pltpu.VMEM((rows, head_dim, keys), F32),
            pltpu.VMEM((rows, head_dim, keys), F32),
        ],
        compiler_params=pltpu.CompilerParams(vmem_limit_bytes=56 * 1024 * 1024),
    )(ids, pair_table, ids, queries, key_side, value_side, attn_out, out_grad, log_norm, bias_all)
    query_grad = lax.psum_scatter(share, "sub", scatter_dimension=3, tiled=True).astype(BF16)
    bias_grad = lax.psum_scatter(running, "row", scatter_dimension=1, tiled=True)
    return (query_grad, key_grad, value_grad, bias_grad)


def solution(mesh):
    return jax.shard_map(
        per_device,
        mesh=mesh,
        in_specs=(
            P("head", ("grp", "row"), None, None),
            P("head", ("grp", "row"), None, "sub"),
            P("head", ("grp", "row"), None, "sub"),
            P("head", ("grp", "row"), None, None),
            P("head", ("grp", "row"), None, None),
            P("head", ("grp", "row"), None),
            P(("grp", "head"), "row", "sub"),
            P("grp"),
            P("grp", None),
        ),
        out_specs=(
            P("head", ("grp", "row"), None, "sub"),
            P("head", ("grp", "row"), None, "sub"),
            P("head", ("grp", "row"), None, "sub"),
            P(("grp", "head"), "row", "sub"),
        ),
        check_vma=False,
    )
```

```python
import functools
import math

import jax
import jax.numpy as jnp
from jax import lax
from jax.experimental import pallas as pl
from jax.experimental.pallas import tpu as pltpu
from jax.sharding import PartitionSpec as P

F32 = jnp.float32
BF16 = jnp.bfloat16
LOG2E = math.log2(math.e)
MASKED = -16384.0
MESH = pl.DeviceIdType.MESH


def three_parts(value):
    high = value.astype(BF16).astype(F32)
    rest = value - high
    mid = rest.astype(BF16).astype(F32)
    return high, mid, rest - mid


def prepare_row(h, i, key_first, row_first, refs):
    k_ref, v_ref, o_ref, do_ref, n_ref, ids_ref, chain_ref, table_ref, aug_ref, rhs_ref = refs
    head_dim, length = o_ref.shape[2], o_ref.shape[3]
    keys = k_ref.shape[3]
    delta = jnp.sum(do_ref[h, i].astype(F32) * o_ref[h, i].astype(F32), axis=0, keepdims=True)
    n1, n2, n3 = three_parts(n_ref[h, pl.ds(i, 1), :] * (-LOG2E))
    d1, d2, d3 = three_parts(-delta)
    line = lax.broadcasted_iota(jnp.int32, (head_dim, length), 0)
    aug = jnp.where(line == 3, 1.0, 0.0)
    for at, part in ((0, n1), (1, n2), (2, n3), (4, d1), (5, d2), (6, d3)):
        aug = jnp.where(line == at, part, aug)
    aug_ref[h, i] = aug.astype(BF16)
    key_chain = chain_ref[:, pl.ds(key_first, keys)]
    row_chain = ids_ref[0, row_first + i]
    seen = jnp.zeros((1, keys), jnp.int32)
    for label in range(table_ref.shape[1]):
        seen = jnp.where(key_chain == label, table_ref[row_chain, label], seen)
    shut = jnp.where(seen == 1, 0.0, MASKED)
    scaled = k_ref[h, i].astype(F32) * (head_dim ** -0.5 * LOG2E)
    high = scaled.astype(BF16)
    low = (scaled - high.astype(F32)).astype(BF16)
    line = lax.broadcasted_iota(jnp.int32, (head_dim, keys), 0)
    score_side = jnp.where(line < 3, 1.0, jnp.where(line == 3, shut, 0.0))
    prob_side = jnp.where((line >= 4) & (line < 7), 1.0, 0.0)
    none = jnp.zeros((head_dim, keys), BF16)
    rhs_ref[h, i, :, :keys] = jnp.concatenate([high, low, none, score_side.astype(BF16)], axis=0)
    rhs_ref[h, i, :, keys:] = jnp.concatenate(
        [none, none, v_ref[h, i], prob_side.astype(BF16)], axis=0
    )


def row_step(h, i, columns, refs):
    q_ref, k_ref, do_ref, aug_ref, rhs_ref, bias_ref, acc_ref, dq_ref, dk_ref, dv_ref = refs
    keys = k_ref.shape[3]
    chunk = min(256, keys)
    query = q_ref[h, i, :, columns]
    grad = do_ref[h, i, :, columns]
    left = jnp.concatenate([query, query, grad, aug_ref[h, i, :, columns]], axis=0).T
    dq = None
    for first in range(0, keys, chunk):
        part = pl.ds(first, chunk)
        scores = jnp.dot(left, rhs_ref[h, i, :, part], preferred_element_type=F32)
        prob_grad = jnp.dot(
            left, rhs_ref[h, i, :, pl.ds(keys + first, chunk)], preferred_element_type=F32
        )
        prob = jnp.exp2(scores + bias_ref[:, part])
        score_grad = prob * prob_grad
        acc_ref[:, part] += score_grad
        low = score_grad.astype(BF16)
        dv_ref[i, :, part] += jnp.dot(grad, prob.astype(BF16), preferred_element_type=F32)
        dk_ref[i, :, part] += jnp.dot(query, low, preferred_element_type=F32)
        share = lax.dot_general(
            k_ref[h, i, :, part], low, (((1,), (1,)), ((), ())), preferred_element_type=F32
        )
        dq = share if dq is None else dq + share
    return dq


def local_kernel(
    ids_ref, table_ref, chain_ref, q_ref, k_ref, v_ref, o_ref, do_ref, n_ref, b_ref,
    dq_ref, dk_ref, dv_ref, db_ref, aug_ref, rhs_ref, bias_ref, dk_acc, dv_acc,
):
    heads, rows, head_dim, length = q_ref.shape
    keys = k_ref.shape[3]
    tile = bias_ref.shape[0]
    factor = head_dim ** -0.5
    key_first = pl.multiple_of(lax.axis_index("sub") * keys, keys)
    row_first = lax.axis_index("row") * rows
    prep = (k_ref, v_ref, o_ref, do_ref, n_ref, ids_ref, chain_ref, table_ref, aug_ref, rhs_ref)

    for h in range(heads):
        @pl.loop(0, rows)
        def _(i):
            prepare_row(h, i, key_first, row_first, prep)

    for h in range(heads):
        dk_acc[...] = jnp.zeros_like(dk_acc)
        dv_acc[...] = jnp.zeros_like(dv_acc)

        @pl.loop(0, length // tile)
        def _(block):
            columns = pl.ds(pl.multiple_of(block * tile, tile), tile)
            bias_ref[...] = b_ref[h, columns, :].astype(F32) * LOG2E
            acc_ref = db_ref.at[h, columns, :]
            acc_ref[...] = jnp.zeros_like(acc_ref)
            refs = (
                q_ref, k_ref, do_ref, aug_ref, rhs_ref, bias_ref, acc_ref, dq_ref, dk_acc, dv_acc
            )

            def body(i, carry):
                dq_ref[h, i, :, columns] = factor * row_step(h, i, columns, refs)
                return carry

            lax.fori_loop(0, rows, body, 0, unroll=2 if rows % 2 == 0 else 1)

        dk_ref[h] = (factor * dk_acc[...]).astype(BF16)
        dv_ref[h] = dv_acc[...].astype(BF16)


def fused_kernel(
    ids_ref, table_ref, chain_ref, q_ref, k_ref, v_ref, o_ref, do_ref, n_ref, b_ref,
    dq_ref, dk_ref, dv_ref, db_ref, aug_ref, rhs_ref, bias_ref, dk_acc, dv_acc,
    shards, totals, leaving, landed, dq_own, dq_peer,
    shard_send, shard_recv, sum_send, sum_recv, dq_send, dq_recv,
):
    heads, rows, head_dim, length = q_ref.shape
    keys = k_ref.shape[3]
    blocks, tile = shards.shape[1], shards.shape[2]
    half_blocks = keys // tile
    factor = head_dim ** -0.5
    me, side = lax.axis_index("row"), lax.axis_index("sub")
    key_first = pl.multiple_of(side * keys, keys)
    above, below = me < blocks - 1, me > 0
    prep = (k_ref, v_ref, o_ref, do_ref, n_ref, ids_ref, chain_ref, table_ref, aug_ref, rhs_ref)

    barrier = pltpu.get_barrier_semaphore()

    def greet(device):
        pl.semaphore_signal(barrier, inc=1, device_id=device, device_id_type=MESH)

    greet({"sub": 1 - side})
    pl.when(above)(lambda: greet({"row": me + 1}))
    pl.when(below)(lambda: greet({"row": me - 1}))
    ends = blocks - 1
    pl.semaphore_wait(barrier, 1 + (2 * ends - 1 - me) // ends + (me + ends - 1) // ends)

    def shard_copy(h, origin, way, source=None):
        return pltpu.make_async_remote_copy(
            src_ref=shards.at[h, origin] if source is None else source,
            dst_ref=shards.at[h, origin],
            send_sem=shard_send.at[h, origin, way],
            recv_sem=shard_recv.at[h, origin],
            device_id={"row": me + 1 - 2 * way},
            device_id_type=MESH,
        )

    def send_own(h):
        pl.when(above)(lambda: shard_copy(h, me, 0, b_ref.at[h]).start())
        pl.when(below)(lambda: shard_copy(h, me, 1, b_ref.at[h]).start())

    def arrive(h, distance):
        @pl.when(me >= distance)
        def _():
            shard_copy(h, me - distance, 0).wait_recv()
            pl.when(above)(lambda: shard_copy(h, me - distance, 0).start())

        @pl.when(me + distance < blocks)
        def _():
            shard_copy(h, me + distance, 1).wait_recv()
            pl.when(below)(lambda: shard_copy(h, me + distance, 1).start())

    def sum_copy(h, block, way):
        return pltpu.make_async_remote_copy(
            src_ref=leaving.at[h, block],
            dst_ref=landed.at[way, h, block],
            send_sem=sum_send.at[h, block],
            recv_sem=sum_recv.at[way, h, block],
            device_id={"row": me + 1 - 2 * way},
            device_id_type=MESH,
        )

    def take(h, block, way):
        sum_copy(h, block, way).wait_recv()
        totals[h, block] += landed[way, h, block].astype(F32)

    def pass_on(h, distance):
        @pl.when(me >= distance)
        def _():
            block = me - distance
            pl.when(above)(lambda: take(h, block, 1))
            leaving[h, block] = totals[h, block].astype(BF16)
            sum_copy(h, block, 1).start()

        @pl.when(me + distance < blocks)
        def _():
            block = me + distance
            pl.when(below)(lambda: take(h, block, 0))
            leaving[h, block] = totals[h, block].astype(BF16)
            sum_copy(h, block, 0).start()

    def finish_sum(h):
        pl.when(above)(lambda: take(h, me, 1))
        pl.when(below)(lambda: take(h, me, 0))
        db_ref[h] = totals[h, me]

    def dq_copy(h, block):
        return pltpu.make_async_remote_copy(
            src_ref=dq_own.at[h, block],
            dst_ref=dq_peer.at[h, block],
            send_sem=dq_send.at[h, block],
            recv_sem=dq_recv.at[h, block],
            device_id={"sub": 1 - side},
            device_id_type=MESH,
        )

    def finish_dq(h):
        for at in range(half_blocks):
            block = side * half_blocks + at
            dq_copy(h, block).wait_recv()
            both = dq_own[h, block] + dq_peer[h, block]
            dq_ref[h, :, :, at * tile : (at + 1) * tile] = (factor * both).astype(BF16)

    send_own(0)
    for h in range(heads):
        shards[h, me] = b_ref[h]

        @pl.loop(0, rows)
        def _(i):
            prepare_row(h, i, key_first, me * rows, prep)

    before = [[] for _ in range(heads * blocks + 1)]
    after = [[] for _ in range(heads * blocks + 1)]
    last = heads * blocks - 1
    for h in range(heads):
        if h:
            before[h].append(functools.partial(send_own, h))
        for distance in range(1, blocks):
            before[h + distance].append(functools.partial(arrive, h, distance))
            step = last - (heads - 1 - h) - distance
            after[step].append(functools.partial(pass_on, h, distance))
        after[last - (heads - 1 - h)].append(functools.partial(finish_sum, h))
        after[min(last, (h + 1) * blocks)].append(functools.partial(finish_dq, h))

    @pl.loop(0, heads * blocks)
    def _(step):
        h = step // blocks
        turn = (1 - h % 2) * (step % blocks) + (h % 2) * (blocks - 1 - step % blocks)
        block = 2 * ((me // 2 + turn // 2) % 2) + (me + turn) % 2
        for at, actions in enumerate(before):
            if actions:
                @pl.when(step == at)
                def _():
                    for action in actions:
                        action()

        @pl.when(step % blocks == 0)
        def _():
            dk_acc[...] = jnp.zeros_like(dk_acc)
            dv_acc[...] = jnp.zeros_like(dv_acc)

        columns = pl.ds(pl.multiple_of(block * tile, tile), tile)
        bias_ref[...] = shards[h, block].astype(F32) * LOG2E
        acc_ref = totals.at[h, block]
        acc_ref[...] = jnp.zeros_like(acc_ref)
        refs = (q_ref, k_ref, do_ref, aug_ref, rhs_ref, bias_ref, acc_ref, None, dk_acc, dv_acc)

        def body(i, carry):
            dq_own[h, block, i] = row_step(h, i, columns, refs)
            return carry

        lax.fori_loop(0, rows, body, 0, unroll=2 if rows % 2 == 0 else 1)
        pl.when(block // half_blocks != side)(lambda: dq_copy(h, block).start())

        @pl.when(step % blocks == blocks - 1)
        def _():
            dk_ref[h] = (factor * dk_acc[...]).astype(BF16)
            dv_ref[h] = dv_acc[...].astype(BF16)

        for at, actions in enumerate(after):
            if actions:
                @pl.when(step == at)
                def _():
                    for action in actions:
                        action()

    for h in range(heads):
        pl.when(above)(lambda: shard_copy(h, me, 0, b_ref.at[h]).wait_send())
        pl.when(below)(lambda: shard_copy(h, me, 1, b_ref.at[h]).wait_send())
        for distance in range(1, blocks):
            @pl.when(me >= distance)
            def _():
                pl.when(above)(lambda: shard_copy(h, me - distance, 0).wait_send())
                sum_copy(h, me - distance, 1).wait_send()

            @pl.when(me + distance < blocks)
            def _():
                pl.when(below)(lambda: shard_copy(h, me + distance, 1).wait_send())
                sum_copy(h, me + distance, 0).wait_send()

        for at in range(half_blocks):
            dq_copy(h, (1 - side) * half_blocks + at).wait_send()


def fused(arrays, ids, pair_table):
    queries, key_side, pair_bias = arrays[0], arrays[1], arrays[6]
    heads, rows, head_dim, length = queries.shape
    keys, tile = key_side.shape[3], pair_bias.shape[1]
    blocks = length // tile
    vmem = pl.BlockSpec(memory_space=pltpu.VMEM)
    smem = pl.BlockSpec(memory_space=pltpu.SMEM)
    dma = pltpu.SemaphoreType.DMA
    return pl.pallas_call(
        fused_kernel,
        out_shape=(
            jax.ShapeDtypeStruct((heads, rows, head_dim, keys), BF16),
            jax.ShapeDtypeStruct((heads, rows, head_dim, keys), BF16),
            jax.ShapeDtypeStruct((heads, rows, head_dim, keys), BF16),
            jax.ShapeDtypeStruct((heads, tile, keys), F32),
        ),
        in_specs=[smem, smem] + [vmem] * 8,
        out_specs=(vmem,) * 4,
        scratch_shapes=[
            pltpu.VMEM((heads, rows, head_dim, length), BF16),
            pltpu.VMEM((heads, rows, 4 * head_dim, 2 * keys), BF16),
            pltpu.VMEM((tile, keys), F32),
            pltpu.VMEM((rows, head_dim, keys), F32),
            pltpu.VMEM((rows, head_dim, keys), F32),
            pltpu.VMEM((heads, blocks, tile, keys), BF16),
            pltpu.VMEM((heads, blocks, tile, keys), F32),
            pltpu.VMEM((heads, blocks, tile, keys), BF16),
            pltpu.VMEM((2, heads, blocks, tile, keys), BF16),
            pltpu.VMEM((heads, blocks, rows, head_dim, tile), F32),
            pltpu.VMEM((heads, blocks, rows, head_dim, tile), F32),
            dma((heads, blocks, 2)),
            dma((heads, blocks)),
            dma((heads, blocks)),
            dma((2, heads, blocks)),
            dma((heads, blocks)),
            dma((heads, blocks)),
        ],
        compiler_params=pltpu.CompilerParams(
            vmem_limit_bytes=58 * 1024 * 1024, collective_id=0, has_side_effects=True
        ),
    )(ids, pair_table, ids, *arrays)


def per_device(
    queries, key_side, value_side, attn_out, out_grad, log_norm, pair_bias, chain_ids, pair_table
):
    heads, rows, head_dim, length = queries.shape
    keys = key_side.shape[3]
    tile = min(256, length)
    ids = chain_ids.reshape(1, length)
    arrays = (queries, key_side, value_side, attn_out, out_grad, log_norm, pair_bias)
    if heads == 2 and lax.axis_size("row") == 4 and pair_bias.shape[1] % 128 == 0:
        return fused(arrays, ids, pair_table)
    bias_all = lax.all_gather(pair_bias, "row", axis=1, tiled=True)
    vmem = pl.BlockSpec(memory_space=pltpu.VMEM)
    smem = pl.BlockSpec(memory_space=pltpu.SMEM)
    share, key_grad, value_grad, running = pl.pallas_call(
        local_kernel,
        out_shape=(
            jax.ShapeDtypeStruct((heads, rows, head_dim, length), F32),
            jax.ShapeDtypeStruct((heads, rows, head_dim, keys), BF16),
            jax.ShapeDtypeStruct((heads, rows, head_dim, keys), BF16),
            jax.ShapeDtypeStruct((heads, length, keys), F32),
        ),
        in_specs=[smem, smem] + [vmem] * 8,
        out_specs=(vmem,) * 4,
        scratch_shapes=[
            pltpu.VMEM((heads, rows, head_dim, length), BF16),
            pltpu.VMEM((heads, rows, 4 * head_dim, 2 * keys), BF16),
            pltpu.VMEM((tile, keys), F32),
            pltpu.VMEM((rows, head_dim, keys), F32),
            pltpu.VMEM((rows, head_dim, keys), F32),
        ],
        compiler_params=pltpu.CompilerParams(vmem_limit_bytes=56 * 1024 * 1024),
    )(ids, pair_table, ids, queries, key_side, value_side, attn_out, out_grad, log_norm, bias_all)
    query_grad = lax.psum_scatter(share, "sub", scatter_dimension=3, tiled=True).astype(BF16)
    bias_grad = lax.psum_scatter(running, "row", scatter_dimension=1, tiled=True)
    return (query_grad, key_grad, value_grad, bias_grad)


def solution(mesh):
    return jax.shard_map(
        per_device,
        mesh=mesh,
        in_specs=(
            P("head", ("grp", "row"), None, None),
            P("head", ("grp", "row"), None, "sub"),
            P("head", ("grp", "row"), None, "sub"),
            P("head", ("grp", "row"), None, None),
            P("head", ("grp", "row"), None, None),
            P("head", ("grp", "row"), None),
            P(("grp", "head"), "row", "sub"),
            P("grp"),
            P("grp", None),
        ),
        out_specs=(
            P("head", ("grp", "row"), None, "sub"),
            P("head", ("grp", "row"), None, "sub"),
            P("head", ("grp", "row"), None, "sub"),
            P(("grp", "head"), "row", "sub"),
        ),
        check_vma=False,
    )
```

```python
import functools
import math

import jax
import jax.numpy as jnp
from jax import lax
from jax.experimental import pallas as pl
from jax.experimental.pallas import tpu as pltpu
from jax.sharding import PartitionSpec as P

F32 = jnp.float32
BF16 = jnp.bfloat16
LOG2E = math.log2(math.e)
MASKED = -16384.0
MESH = pl.DeviceIdType.MESH


def three_parts(value):
    high = value.astype(BF16).astype(F32)
    rest = value - high
    mid = rest.astype(BF16).astype(F32)
    return high, mid, rest - mid


def prepare_row(h, i, key_first, row_first, refs):
    k_ref, v_ref, o_ref, do_ref, n_ref, ids_ref, chain_ref, table_ref, aug_ref, rhs_ref = refs
    head_dim, length = o_ref.shape[2], o_ref.shape[3]
    keys = k_ref.shape[3]
    delta = jnp.sum(do_ref[h, i].astype(F32) * o_ref[h, i].astype(F32), axis=0, keepdims=True)
    n1, n2, n3 = three_parts(n_ref[h, pl.ds(i, 1), :] * (-LOG2E))
    d1, d2, d3 = three_parts(-delta)
    line = lax.broadcasted_iota(jnp.int32, (head_dim, length), 0)
    aug = jnp.where(line == 3, 1.0, 0.0)
    for at, part in ((0, n1), (1, n2), (2, n3), (4, d1), (5, d2), (6, d3)):
        aug = jnp.where(line == at, part, aug)
    aug_ref[h, i] = aug.astype(BF16)
    key_chain = chain_ref[:, pl.ds(key_first, keys)]
    row_chain = ids_ref[0, row_first + i]
    seen = jnp.zeros((1, keys), jnp.int32)
    for label in range(table_ref.shape[1]):
        seen = jnp.where(key_chain == label, table_ref[row_chain, label], seen)
    shut = jnp.where(seen == 1, 0.0, MASKED)
    scaled = k_ref[h, i].astype(F32) * (head_dim ** -0.5 * LOG2E)
    high = scaled.astype(BF16)
    low = (scaled - high.astype(F32)).astype(BF16)
    line = lax.broadcasted_iota(jnp.int32, (head_dim, keys), 0)
    score_side = jnp.where(line < 3, 1.0, jnp.where(line == 3, shut, 0.0))
    prob_side = jnp.where((line >= 4) & (line < 7), 1.0, 0.0)
    none = jnp.zeros((head_dim, keys), BF16)
    rhs_ref[h, i, :, :keys] = jnp.concatenate([high, low, none, score_side.astype(BF16)], axis=0)
    rhs_ref[h, i, :, keys:] = jnp.concatenate(
        [none, none, v_ref[h, i], prob_side.astype(BF16)], axis=0
    )


def row_step(h, i, columns, refs):
    q_ref, k_ref, do_ref, aug_ref, rhs_ref, bias_ref, acc_ref, dq_ref, dk_ref, dv_ref = refs
    keys = k_ref.shape[3]
    chunk = min(512, keys)
    query = q_ref[h, i, :, columns]
    grad = do_ref[h, i, :, columns]
    left = jnp.concatenate([query, query, grad, aug_ref[h, i, :, columns]], axis=0).T
    dq = None
    for first in range(0, keys, chunk):
        part = pl.ds(first, chunk)
        scores = jnp.dot(left, rhs_ref[h, i, :, part], preferred_element_type=F32)
        prob_grad = jnp.dot(
            left, rhs_ref[h, i, :, pl.ds(keys + first, chunk)], preferred_element_type=F32
        )
        prob = jnp.exp2(scores + bias_ref[:, part])
        score_grad = prob * prob_grad
        acc_ref[:, part] += score_grad
        low = score_grad.astype(BF16)
        dv_ref[i, :, part] += jnp.dot(grad, prob.astype(BF16), preferred_element_type=F32)
        dk_ref[i, :, part] += jnp.dot(query, low, preferred_element_type=F32)
        share = lax.dot_general(
            k_ref[h, i, :, part], low, (((1,), (1,)), ((), ())), preferred_element_type=F32
        )
        dq = share if dq is None else dq + share
    return dq


def local_kernel(
    ids_ref, table_ref, chain_ref, q_ref, k_ref, v_ref, o_ref, do_ref, n_ref, b_ref,
    dq_ref, dk_ref, dv_ref, db_ref, aug_ref, rhs_ref, bias_ref, dk_acc, dv_acc,
):
    heads, rows, head_dim, length = q_ref.shape
    keys = k_ref.shape[3]
    tile = bias_ref.shape[0]
    factor = head_dim ** -0.5
    key_first = pl.multiple_of(lax.axis_index("sub") * keys, keys)
    row_first = lax.axis_index("row") * rows
    prep = (k_ref, v_ref, o_ref, do_ref, n_ref, ids_ref, chain_ref, table_ref, aug_ref, rhs_ref)

    for h in range(heads):
        @pl.loop(0, rows)
        def _(i):
            prepare_row(h, i, key_first, row_first, prep)

    for h in range(heads):
        dk_acc[...] = jnp.zeros_like(dk_acc)
        dv_acc[...] = jnp.zeros_like(dv_acc)

        @pl.loop(0, length // tile)
        def _(block):
            columns = pl.ds(pl.multiple_of(block * tile, tile), tile)
            bias_ref[...] = b_ref[h, columns, :].astype(F32) * LOG2E
            acc_ref = db_ref.at[h, columns, :]
            acc_ref[...] = jnp.zeros_like(acc_ref)
            refs = (
                q_ref, k_ref, do_ref, aug_ref, rhs_ref, bias_ref, acc_ref, dq_ref, dk_acc, dv_acc
            )

            def body(i, carry):
                dq_ref[h, i, :, columns] = factor * row_step(h, i, columns, refs)
                return carry

            lax.fori_loop(0, rows, body, 0, unroll=2 if rows % 2 == 0 else 1)

        dk_ref[h] = (factor * dk_acc[...]).astype(BF16)
        dv_ref[h] = dv_acc[...].astype(BF16)


def fused_kernel(
    ids_ref, table_ref, chain_ref, q_ref, k_ref, v_ref, o_ref, do_ref, n_ref, b_ref,
    dq_ref, dk_ref, dv_ref, db_ref, aug_ref, rhs_ref, bias_ref, dk_acc, dv_acc,
    shards, totals, leaving, landed, dq_own, dq_peer,
    shard_send, shard_recv, sum_send, sum_recv, dq_send, dq_recv,
):
    heads, rows, head_dim, length = q_ref.shape
    keys = k_ref.shape[3]
    blocks, tile = shards.shape[1], shards.shape[2]
    half_blocks = keys // tile
    factor = head_dim ** -0.5
    me, side = lax.axis_index("row"), lax.axis_index("sub")
    key_first = pl.multiple_of(side * keys, keys)
    above, below = me < blocks - 1, me > 0
    prep = (k_ref, v_ref, o_ref, do_ref, n_ref, ids_ref, chain_ref, table_ref, aug_ref, rhs_ref)

    barrier = pltpu.get_barrier_semaphore()

    def greet(device):
        pl.semaphore_signal(barrier, inc=1, device_id=device, device_id_type=MESH)

    greet({"sub": 1 - side})
    pl.when(above)(lambda: greet({"row": me + 1}))
    pl.when(below)(lambda: greet({"row": me - 1}))
    ends = blocks - 1
    pl.semaphore_wait(barrier, 1 + (2 * ends - 1 - me) // ends + (me + ends - 1) // ends)

    def shard_copy(h, origin, way, source=None):
        return pltpu.make_async_remote_copy(
            src_ref=shards.at[h, origin] if source is None else source,
            dst_ref=shards.at[h, origin],
            send_sem=shard_send.at[h, origin, way],
            recv_sem=shard_recv.at[h, origin],
            device_id={"row": me + 1 - 2 * way},
            device_id_type=MESH,
        )

    def send_own(h):
        pl.when(above)(lambda: shard_copy(h, me, 0, b_ref.at[h]).start())
        pl.when(below)(lambda: shard_copy(h, me, 1, b_ref.at[h]).start())

    def arrive(h, distance):
        @pl.when(me >= distance)
        def _():
            shard_copy(h, me - distance, 0).wait_recv()
            pl.when(above)(lambda: shard_copy(h, me - distance, 0).start())

        @pl.when(me + distance < blocks)
        def _():
            shard_copy(h, me + distance, 1).wait_recv()
            pl.when(below)(lambda: shard_copy(h, me + distance, 1).start())

    def sum_copy(h, block, way):
        return pltpu.make_async_remote_copy(
            src_ref=leaving.at[h, block],
            dst_ref=landed.at[way, h, block],
            send_sem=sum_send.at[h, block],
            recv_sem=sum_recv.at[way, h, block],
            device_id={"row": me + 1 - 2 * way},
            device_id_type=MESH,
        )

    def take(h, block, way):
        sum_copy(h, block, way).wait_recv()
        totals[h, block] += landed[way, h, block].astype(F32)

    def pass_on(h, distance):
        @pl.when(me >= distance)
        def _():
            block = me - distance
            pl.when(above)(lambda: take(h, block, 1))
            leaving[h, block] = totals[h, block].astype(BF16)
            sum_copy(h, block, 1).start()

        @pl.when(me + distance < blocks)
        def _():
            block = me + distance
            pl.when(below)(lambda: take(h, block, 0))
            leaving[h, block] = totals[h, block].astype(BF16)
            sum_copy(h, block, 0).start()

    def finish_sum(h):
        pl.when(above)(lambda: take(h, me, 1))
        pl.when(below)(lambda: take(h, me, 0))
        db_ref[h] = totals[h, me]

    def dq_copy(h, block):
        return pltpu.make_async_remote_copy(
            src_ref=dq_own.at[h, block],
            dst_ref=dq_peer.at[h, block],
            send_sem=dq_send.at[h, block],
            recv_sem=dq_recv.at[h, block],
            device_id={"sub": 1 - side},
            device_id_type=MESH,
        )

    def finish_dq(h):
        for at in range(half_blocks):
            block = side * half_blocks + at
            dq_copy(h, block).wait_recv()
            both = dq_own[h, block] + dq_peer[h, block]
            dq_ref[h, :, :, at * tile : (at + 1) * tile] = (factor * both).astype(BF16)

    send_own(0)
    for h in range(heads):
        shards[h, me] = b_ref[h]

        @pl.loop(0, rows)
        def _(i):
            prepare_row(h, i, key_first, me * rows, prep)

    before = {
        2: [(arrive, 0, 1)],
        3: [(send_own, 1)],
        4: [(arrive, 0, 2)],
        6: [(arrive, 0, 3), (arrive, 1, 1)],
        8: [(arrive, 1, 2)],
        10: [(arrive, 1, 3)],
    }
    after = {
        7: [(pass_on, 0, 3)],
        9: [(pass_on, 0, 2)],
        11: [(pass_on, 1, 3), (pass_on, 0, 1)],
        13: [(pass_on, 1, 2)],
        14: [(finish_dq, 0)],
        15: [(pass_on, 1, 1), (finish_sum, 0), (finish_dq, 1), (finish_sum, 1)],
    }

    def run(plan, half_step):
        for at, actions in plan.items():
            @pl.when(half_step == at)
            def _():
                for action, *what in actions:
                    action(*what)

    half_rows = rows // 2

    @pl.loop(0, 2 * heads * blocks)
    def _(half_step):
        step = half_step // 2
        h, turn = step // blocks, step % blocks
        turn = (1 - h) * turn + h * (2 * (1 - turn // 2) + (turn + turn // 2) % 2)
        block = 2 * ((me // 2 + turn // 2) % 2) + (me + turn) % 2
        run(before, half_step)

        @pl.when(half_step % (2 * blocks) == 0)
        def _():
            dk_acc[...] = jnp.zeros_like(dk_acc)
            dv_acc[...] = jnp.zeros_like(dv_acc)

        columns = pl.ds(pl.multiple_of(block * tile, tile), tile)
        acc_ref = totals.at[h, block]

        @pl.when(half_step % 2 == 0)
        def _():
            bias_ref[...] = shards[h, block].astype(F32) * LOG2E
            acc_ref[...] = jnp.zeros_like(acc_ref)

        refs = (q_ref, k_ref, do_ref, aug_ref, rhs_ref, bias_ref, acc_ref, None, dk_acc, dv_acc)
        first = half_step % 2 * half_rows

        def body(i, carry):
            dq_own[h, block, first + i] = row_step(h, first + i, columns, refs)
            return carry

        lax.fori_loop(0, half_rows, body, 0, unroll=6 if half_rows % 6 == 0 else 1)

        @pl.when((half_step % 2 == 1) & (block // half_blocks != side))
        def _():
            dq_copy(h, block).start()

        @pl.when(half_step % (2 * blocks) == 2 * blocks - 1)
        def _():
            dk_ref[h] = (factor * dk_acc[...]).astype(BF16)
            dv_ref[h] = dv_acc[...].astype(BF16)

        run(after, half_step)

    for h in range(heads):
        pl.when(above)(lambda: shard_copy(h, me, 0, b_ref.at[h]).wait_send())
        pl.when(below)(lambda: shard_copy(h, me, 1, b_ref.at[h]).wait_send())
        for distance in range(1, blocks):
            @pl.when(me >= distance)
            def _():
                pl.when(above)(lambda: shard_copy(h, me - distance, 0).wait_send())
                sum_copy(h, me - distance, 1).wait_send()

            @pl.when(me + distance < blocks)
            def _():
                pl.when(below)(lambda: shard_copy(h, me + distance, 1).wait_send())
                sum_copy(h, me + distance, 0).wait_send()

        for at in range(half_blocks):
            dq_copy(h, (1 - side) * half_blocks + at).wait_send()


def fused(arrays, ids, pair_table):
    queries, key_side, pair_bias = arrays[0], arrays[1], arrays[6]
    heads, rows, head_dim, length = queries.shape
    keys, tile = key_side.shape[3], pair_bias.shape[1]
    blocks = length // tile
    vmem = pl.BlockSpec(memory_space=pltpu.VMEM)
    smem = pl.BlockSpec(memory_space=pltpu.SMEM)
    dma = pltpu.SemaphoreType.DMA
    return pl.pallas_call(
        fused_kernel,
        out_shape=(
            jax.ShapeDtypeStruct((heads, rows, head_dim, keys), BF16),
            jax.ShapeDtypeStruct((heads, rows, head_dim, keys), BF16),
            jax.ShapeDtypeStruct((heads, rows, head_dim, keys), BF16),
            jax.ShapeDtypeStruct((heads, tile, keys), F32),
        ),
        in_specs=[smem, smem] + [vmem] * 8,
        out_specs=(vmem,) * 4,
        scratch_shapes=[
            pltpu.VMEM((heads, rows, head_dim, length), BF16),
            pltpu.VMEM((heads, rows, 4 * head_dim, 2 * keys), BF16),
            pltpu.VMEM((tile, keys), F32),
            pltpu.VMEM((rows, head_dim, keys), F32),
            pltpu.VMEM((rows, head_dim, keys), F32),
            pltpu.VMEM((heads, blocks, tile, keys), BF16),
            pltpu.VMEM((heads, blocks, tile, keys), F32),
            pltpu.VMEM((heads, blocks, tile, keys), BF16),
            pltpu.VMEM((2, heads, blocks, tile, keys), BF16),
            pltpu.VMEM((heads, blocks, rows, head_dim, tile), F32),
            pltpu.VMEM((heads, blocks, rows, head_dim, tile), F32),
            dma((heads, blocks, 2)),
            dma((heads, blocks)),
            dma((heads, blocks)),
            dma((2, heads, blocks)),
            dma((heads, blocks)),
            dma((heads, blocks)),
        ],
        compiler_params=pltpu.CompilerParams(
            vmem_limit_bytes=58 * 1024 * 1024, collective_id=0, has_side_effects=True
        ),
    )(ids, pair_table, ids, *arrays)


def per_device(
    queries, key_side, value_side, attn_out, out_grad, log_norm, pair_bias, chain_ids, pair_table
):
    heads, rows, head_dim, length = queries.shape
    keys = key_side.shape[3]
    tile = min(256, length)
    ids = chain_ids.reshape(1, length)
    arrays = (queries, key_side, value_side, attn_out, out_grad, log_norm, pair_bias)
    if heads == 2 and rows % 2 == 0 and lax.axis_size("row") == 4 and pair_bias.shape[1] % 128 == 0:
        return fused(arrays, ids, pair_table)
    bias_all = lax.all_gather(pair_bias, "row", axis=1, tiled=True)
    vmem = pl.BlockSpec(memory_space=pltpu.VMEM)
    smem = pl.BlockSpec(memory_space=pltpu.SMEM)
    share, key_grad, value_grad, running = pl.pallas_call(
        local_kernel,
        out_shape=(
            jax.ShapeDtypeStruct((heads, rows, head_dim, length), F32),
            jax.ShapeDtypeStruct((heads, rows, head_dim, keys), BF16),
            jax.ShapeDtypeStruct((heads, rows, head_dim, keys), BF16),
            jax.ShapeDtypeStruct((heads, length, keys), F32),
        ),
        in_specs=[smem, smem] + [vmem] * 8,
        out_specs=(vmem,) * 4,
        scratch_shapes=[
            pltpu.VMEM((heads, rows, head_dim, length), BF16),
            pltpu.VMEM((heads, rows, 4 * head_dim, 2 * keys), BF16),
            pltpu.VMEM((tile, keys), F32),
            pltpu.VMEM((rows, head_dim, keys), F32),
            pltpu.VMEM((rows, head_dim, keys), F32),
        ],
        compiler_params=pltpu.CompilerParams(vmem_limit_bytes=56 * 1024 * 1024),
    )(ids, pair_table, ids, queries, key_side, value_side, attn_out, out_grad, log_norm, bias_all)
    query_grad = lax.psum_scatter(share, "sub", scatter_dimension=3, tiled=True).astype(BF16)
    bias_grad = lax.psum_scatter(running, "row", scatter_dimension=1, tiled=True)
    return (query_grad, key_grad, value_grad, bias_grad)


def solution(mesh):
    return jax.shard_map(
        per_device,
        mesh=mesh,
        in_specs=(
            P("head", ("grp", "row"), None, None),
            P("head", ("grp", "row"), None, "sub"),
            P("head", ("grp", "row"), None, "sub"),
            P("head", ("grp", "row"), None, None),
            P("head", ("grp", "row"), None, None),
            P("head", ("grp", "row"), None),
            P(("grp", "head"), "row", "sub"),
            P("grp"),
            P("grp", None),
        ),
        out_specs=(
            P("head", ("grp", "row"), None, "sub"),
            P("head", ("grp", "row"), None, "sub"),
            P("head", ("grp", "row"), None, "sub"),
            P(("grp", "head"), "row", "sub"),
        ),
        check_vma=False,
    )
```

```python
import functools
import math

import jax
import jax.numpy as jnp
from jax import lax
from jax.experimental import pallas as pl
from jax.experimental.pallas import tpu as pltpu
from jax.sharding import PartitionSpec as P

F32 = jnp.float32
BF16 = jnp.bfloat16
LOG2E = math.log2(math.e)
MASKED = -16384.0
MESH = pl.DeviceIdType.MESH


def three_parts(value):
    high = value.astype(BF16).astype(F32)
    rest = value - high
    mid = rest.astype(BF16).astype(F32)
    return high, mid, rest - mid


def prepare_row(h, i, key_first, row_first, refs):
    k_ref, v_ref, o_ref, do_ref, n_ref, ids_ref, chain_ref, table_ref, aug_ref, rhs_ref = refs
    head_dim, length = o_ref.shape[2], o_ref.shape[3]
    keys = k_ref.shape[3]
    delta = jnp.sum(do_ref[h, i].astype(F32) * o_ref[h, i].astype(F32), axis=0, keepdims=True)
    n1, n2, n3 = three_parts(n_ref[h, pl.ds(i, 1), :] * (-LOG2E))
    d1, d2, d3 = three_parts(-delta)
    line = lax.broadcasted_iota(jnp.int32, (head_dim, length), 0)
    aug = jnp.where(line == 3, 1.0, 0.0)
    for at, part in ((0, n1), (1, n2), (2, n3), (4, d1), (5, d2), (6, d3)):
        aug = jnp.where(line == at, part, aug)
    aug_ref[h, i] = aug.astype(BF16)
    key_chain = chain_ref[:, pl.ds(key_first, keys)]
    row_chain = ids_ref[0, row_first + i]
    seen = jnp.zeros((1, keys), jnp.int32)
    for label in range(table_ref.shape[1]):
        seen = jnp.where(key_chain == label, table_ref[row_chain, label], seen)
    shut = jnp.where(seen == 1, 0.0, MASKED)
    scaled = k_ref[h, i].astype(F32) * (head_dim ** -0.5 * LOG2E)
    high = scaled.astype(BF16)
    low = (scaled - high.astype(F32)).astype(BF16)
    line = lax.broadcasted_iota(jnp.int32, (head_dim, keys), 0)
    score_side = jnp.where(line < 3, 1.0, jnp.where(line == 3, shut, 0.0))
    prob_side = jnp.where((line >= 4) & (line < 7), 1.0, 0.0)
    none = jnp.zeros((head_dim, keys), BF16)
    rhs_ref[h, i, :, :keys] = jnp.concatenate([high, low, none, score_side.astype(BF16)], axis=0)
    rhs_ref[h, i, :, keys:] = jnp.concatenate(
        [none, none, v_ref[h, i], prob_side.astype(BF16)], axis=0
    )


def row_step(h, i, columns, refs):
    q_ref, k_ref, do_ref, aug_ref, rhs_ref, bias_ref, acc_ref, dq_ref, dk_ref, dv_ref = refs
    keys = k_ref.shape[3]
    chunk = min(512, keys)
    query = q_ref[h, i, :, columns]
    grad = do_ref[h, i, :, columns]
    left = jnp.concatenate([query, query, grad, aug_ref[h, i, :, columns]], axis=0).T
    dq = None
    for first in range(0, keys, chunk):
        part = pl.ds(first, chunk)
        scores = jnp.dot(left, rhs_ref[h, i, :, part], preferred_element_type=F32)
        prob_grad = jnp.dot(
            left, rhs_ref[h, i, :, pl.ds(keys + first, chunk)], preferred_element_type=F32
        )
        prob = jnp.exp2(scores + bias_ref[:, part])
        score_grad = prob * prob_grad
        acc_ref[:, part] += score_grad
        low = score_grad.astype(BF16)
        dv_ref[i, :, part] += jnp.dot(grad, prob.astype(BF16), preferred_element_type=F32)
        dk_ref[i, :, part] += jnp.dot(query, low, preferred_element_type=F32)
        share = lax.dot_general(
            k_ref[h, i, :, part], low, (((1,), (1,)), ((), ())), preferred_element_type=F32
        )
        dq = share if dq is None else dq + share
    return dq


def local_kernel(
    ids_ref, table_ref, chain_ref, q_ref, k_ref, v_ref, o_ref, do_ref, n_ref, b_ref,
    dq_ref, dk_ref, dv_ref, db_ref, aug_ref, rhs_ref, bias_ref, dk_acc, dv_acc,
):
    heads, rows, head_dim, length = q_ref.shape
    keys = k_ref.shape[3]
    tile = bias_ref.shape[0]
    factor = head_dim ** -0.5
    key_first = pl.multiple_of(lax.axis_index("sub") * keys, keys)
    row_first = lax.axis_index("row") * rows
    prep = (k_ref, v_ref, o_ref, do_ref, n_ref, ids_ref, chain_ref, table_ref, aug_ref, rhs_ref)

    for h in range(heads):
        @pl.loop(0, rows)
        def _(i):
            prepare_row(h, i, key_first, row_first, prep)

    for h in range(heads):
        dk_acc[...] = jnp.zeros_like(dk_acc)
        dv_acc[...] = jnp.zeros_like(dv_acc)

        @pl.loop(0, length // tile)
        def _(block):
            columns = pl.ds(pl.multiple_of(block * tile, tile), tile)
            bias_ref[...] = b_ref[h, columns, :].astype(F32) * LOG2E
            acc_ref = db_ref.at[h, columns, :]
            acc_ref[...] = jnp.zeros_like(acc_ref)
            refs = (
                q_ref, k_ref, do_ref, aug_ref, rhs_ref, bias_ref, acc_ref, dq_ref, dk_acc, dv_acc
            )

            def body(i, carry):
                dq_ref[h, i, :, columns] = factor * row_step(h, i, columns, refs)
                return carry

            lax.fori_loop(0, rows, body, 0, unroll=2 if rows % 2 == 0 else 1)

        dk_ref[h] = (factor * dk_acc[...]).astype(BF16)
        dv_ref[h] = dv_acc[...].astype(BF16)


def fused_kernel(
    ids_ref, table_ref, chain_ref, q_ref, k_ref, v_ref, o_ref, do_ref, n_ref, b_ref,
    dq_ref, dk_ref, dv_ref, db_ref, aug_ref, rhs_ref, bias_ref, dk_acc, dv_acc,
    shards, totals, leaving, landed, dq_own, dq_peer,
    shard_send, shard_recv, sum_send, sum_recv, dq_send, dq_recv,
):
    heads, rows, head_dim, length = q_ref.shape
    keys = k_ref.shape[3]
    blocks, tile = shards.shape[1], shards.shape[2]
    half_blocks = keys // tile
    factor = head_dim ** -0.5
    me, side = lax.axis_index("row"), lax.axis_index("sub")
    key_first = pl.multiple_of(side * keys, keys)
    above, below = me < blocks - 1, me > 0
    prep = (k_ref, v_ref, o_ref, do_ref, n_ref, ids_ref, chain_ref, table_ref, aug_ref, rhs_ref)

    barrier = pltpu.get_barrier_semaphore()

    def greet(device):
        pl.semaphore_signal(barrier, inc=1, device_id=device, device_id_type=MESH)

    greet({"sub": 1 - side})
    pl.when(above)(lambda: greet({"row": me + 1}))
    pl.when(below)(lambda: greet({"row": me - 1}))
    ends = blocks - 1
    pl.semaphore_wait(barrier, 1 + (2 * ends - 1 - me) // ends + (me + ends - 1) // ends)

    def shard_copy(h, origin, way, source=None):
        return pltpu.make_async_remote_copy(
            src_ref=shards.at[h, origin] if source is None else source,
            dst_ref=shards.at[h, origin],
            send_sem=shard_send.at[h, origin, way],
            recv_sem=shard_recv.at[h, origin],
            device_id={"row": me + 1 - 2 * way},
            device_id_type=MESH,
        )

    def send_own(h):
        pl.when(above)(lambda: shard_copy(h, me, 0, b_ref.at[h]).start())
        pl.when(below)(lambda: shard_copy(h, me, 1, b_ref.at[h]).start())

    def arrive(h, distance):
        @pl.when(me >= distance)
        def _():
            shard_copy(h, me - distance, 0).wait_recv()
            pl.when(above)(lambda: shard_copy(h, me - distance, 0).start())

        @pl.when(me + distance < blocks)
        def _():
            shard_copy(h, me + distance, 1).wait_recv()
            pl.when(below)(lambda: shard_copy(h, me + distance, 1).start())

    def sum_copy(h, block, way):
        return pltpu.make_async_remote_copy(
            src_ref=leaving.at[h, block],
            dst_ref=landed.at[way, h, block],
            send_sem=sum_send.at[h, block],
            recv_sem=sum_recv.at[way, h, block],
            device_id={"row": me + 1 - 2 * way},
            device_id_type=MESH,
        )

    def take(h, block, way):
        sum_copy(h, block, way).wait_recv()
        totals[h, block] += landed[way, h, block].astype(F32)

    def pass_on(h, distance):
        @pl.when(me >= distance)
        def _():
            block = me - distance
            pl.when(above)(lambda: take(h, block, 1))
            leaving[h, block] = totals[h, block].astype(BF16)
            sum_copy(h, block, 1).start()

        @pl.when(me + distance < blocks)
        def _():
            block = me + distance
            pl.when(below)(lambda: take(h, block, 0))
            leaving[h, block] = totals[h, block].astype(BF16)
            sum_copy(h, block, 0).start()

    def finish_sum(h):
        pl.when(above)(lambda: take(h, me, 1))
        pl.when(below)(lambda: take(h, me, 0))
        db_ref[h] = totals[h, me]

    def dq_copy(h, block):
        return pltpu.make_async_remote_copy(
            src_ref=dq_own.at[h, block],
            dst_ref=dq_peer.at[h, block],
            send_sem=dq_send.at[h, block],
            recv_sem=dq_recv.at[h, block],
            device_id={"sub": 1 - side},
            device_id_type=MESH,
        )

    def finish_dq(h):
        for at in range(half_blocks):
            block = side * half_blocks + at
            dq_copy(h, block).wait_recv()
            both = dq_own[h, block] + dq_peer[h, block]
            dq_ref[h, :, :, at * tile : (at + 1) * tile] = (factor * both).astype(BF16)

    send_own(0)
    for h in range(heads):
        shards[h, me] = b_ref[h]

        @pl.loop(0, rows)
        def _(i):
            prepare_row(h, i, key_first, me * rows, prep)

    before = {
        1: [(arrive, 0, 1)],
        2: [(send_own, 1)],
        4: [(arrive, 0, 2)],
        5: [(arrive, 1, 1)],
        6: [(arrive, 0, 3)],
        8: [(arrive, 1, 2)],
        10: [(arrive, 1, 3)],
    }
    after = {
        7: [(pass_on, 0, 3)],
        9: [(pass_on, 0, 2)],
        11: [(pass_on, 1, 3), (pass_on, 0, 1)],
        13: [(pass_on, 1, 2)],
        14: [(finish_dq, 0)],
        15: [(pass_on, 1, 1), (finish_sum, 0), (finish_dq, 1), (finish_sum, 1)],
    }

    def run(plan, half_step):
        for at, actions in plan.items():
            @pl.when(half_step == at)
            def _():
                for action, *what in actions:
                    action(*what)

    half_rows = rows // 2

    @pl.loop(0, 2 * heads * blocks)
    def _(half_step):
        step = half_step // 2
        h, turn = step // blocks, step % blocks
        turn = (1 - h) * turn + h * (2 * (1 - turn // 2) + (turn + turn // 2) % 2)
        block = 2 * ((me // 2 + turn // 2) % 2) + (me + turn) % 2
        run(before, half_step)

        @pl.when(half_step % (2 * blocks) == 0)
        def _():
            dk_acc[...] = jnp.zeros_like(dk_acc)
            dv_acc[...] = jnp.zeros_like(dv_acc)

        columns = pl.ds(pl.multiple_of(block * tile, tile), tile)
        acc_ref = totals.at[h, block]

        @pl.when(half_step % 2 == 0)
        def _():
            bias_ref[...] = shards[h, block].astype(F32) * LOG2E
            acc_ref[...] = jnp.zeros_like(acc_ref)

        refs = (q_ref, k_ref, do_ref, aug_ref, rhs_ref, bias_ref, acc_ref, None, dk_acc, dv_acc)
        first = half_step % 2 * half_rows

        def body(i, carry):
            dq_own[h, block, first + i] = row_step(h, first + i, columns, refs)
            return carry

        lax.fori_loop(0, half_rows, body, 0, unroll=6 if half_rows % 6 == 0 else 1)

        @pl.when((half_step % 2 == 1) & (block // half_blocks != side))
        def _():
            dq_copy(h, block).start()

        @pl.when(half_step % (2 * blocks) == 2 * blocks - 1)
        def _():
            dk_ref[h] = (factor * dk_acc[...]).astype(BF16)
            dv_ref[h] = dv_acc[...].astype(BF16)

        run(after, half_step)

    for h in range(heads):
        pl.when(above)(lambda: shard_copy(h, me, 0, b_ref.at[h]).wait_send())
        pl.when(below)(lambda: shard_copy(h, me, 1, b_ref.at[h]).wait_send())
        for distance in range(1, blocks):
            @pl.when(me >= distance)
            def _():
                pl.when(above)(lambda: shard_copy(h, me - distance, 0).wait_send())
                sum_copy(h, me - distance, 1).wait_send()

            @pl.when(me + distance < blocks)
            def _():
                pl.when(below)(lambda: shard_copy(h, me + distance, 1).wait_send())
                sum_copy(h, me + distance, 0).wait_send()

        for at in range(half_blocks):
            dq_copy(h, (1 - side) * half_blocks + at).wait_send()


def fused(arrays, ids, pair_table):
    queries, key_side, pair_bias = arrays[0], arrays[1], arrays[6]
    heads, rows, head_dim, length = queries.shape
    keys, tile = key_side.shape[3], pair_bias.shape[1]
    blocks = length // tile
    vmem = pl.BlockSpec(memory_space=pltpu.VMEM)
    smem = pl.BlockSpec(memory_space=pltpu.SMEM)
    dma = pltpu.SemaphoreType.DMA
    return pl.pallas_call(
        fused_kernel,
        out_shape=(
            jax.ShapeDtypeStruct((heads, rows, head_dim, keys), BF16),
            jax.ShapeDtypeStruct((heads, rows, head_dim, keys), BF16),
            jax.ShapeDtypeStruct((heads, rows, head_dim, keys), BF16),
            jax.ShapeDtypeStruct((heads, tile, keys), F32),
        ),
        in_specs=[smem, smem] + [vmem] * 8,
        out_specs=(vmem,) * 4,
        scratch_shapes=[
            pltpu.VMEM((heads, rows, head_dim, length), BF16),
            pltpu.VMEM((heads, rows, 4 * head_dim, 2 * keys), BF16),
            pltpu.VMEM((tile, keys), F32),
            pltpu.VMEM((rows, head_dim, keys), F32),
            pltpu.VMEM((rows, head_dim, keys), F32),
            pltpu.VMEM((heads, blocks, tile, keys), BF16),
            pltpu.VMEM((heads, blocks, tile, keys), F32),
            pltpu.VMEM((heads, blocks, tile, keys), BF16),
            pltpu.VMEM((2, heads, blocks, tile, keys), BF16),
            pltpu.VMEM((heads, blocks, rows, head_dim, tile), F32),
            pltpu.VMEM((heads, blocks, rows, head_dim, tile), F32),
            dma((heads, blocks, 2)),
            dma((heads, blocks)),
            dma((heads, blocks)),
            dma((2, heads, blocks)),
            dma((heads, blocks)),
            dma((heads, blocks)),
        ],
        compiler_params=pltpu.CompilerParams(
            vmem_limit_bytes=58 * 1024 * 1024, collective_id=0, has_side_effects=True
        ),
    )(ids, pair_table, ids, *arrays)


def per_device(
    queries, key_side, value_side, attn_out, out_grad, log_norm, pair_bias, chain_ids, pair_table
):
    heads, rows, head_dim, length = queries.shape
    keys = key_side.shape[3]
    tile = min(256, length)
    ids = chain_ids.reshape(1, length)
    arrays = (queries, key_side, value_side, attn_out, out_grad, log_norm, pair_bias)
    if heads == 2 and rows % 2 == 0 and lax.axis_size("row") == 4 and pair_bias.shape[1] % 128 == 0:
        return fused(arrays, ids, pair_table)
    bias_all = lax.all_gather(pair_bias, "row", axis=1, tiled=True)
    vmem = pl.BlockSpec(memory_space=pltpu.VMEM)
    smem = pl.BlockSpec(memory_space=pltpu.SMEM)
    share, key_grad, value_grad, running = pl.pallas_call(
        local_kernel,
        out_shape=(
            jax.ShapeDtypeStruct((heads, rows, head_dim, length), F32),
            jax.ShapeDtypeStruct((heads, rows, head_dim, keys), BF16),
            jax.ShapeDtypeStruct((heads, rows, head_dim, keys), BF16),
            jax.ShapeDtypeStruct((heads, length, keys), F32),
        ),
        in_specs=[smem, smem] + [vmem] * 8,
        out_specs=(vmem,) * 4,
        scratch_shapes=[
            pltpu.VMEM((heads, rows, head_dim, length), BF16),
            pltpu.VMEM((heads, rows, 4 * head_dim, 2 * keys), BF16),
            pltpu.VMEM((tile, keys), F32),
            pltpu.VMEM((rows, head_dim, keys), F32),
            pltpu.VMEM((rows, head_dim, keys), F32),
        ],
        compiler_params=pltpu.CompilerParams(vmem_limit_bytes=56 * 1024 * 1024),
    )(ids, pair_table, ids, queries, key_side, value_side, attn_out, out_grad, log_norm, bias_all)
    query_grad = lax.psum_scatter(share, "sub", scatter_dimension=3, tiled=True).astype(BF16)
    bias_grad = lax.psum_scatter(running, "row", scatter_dimension=1, tiled=True)
    return (query_grad, key_grad, value_grad, bias_grad)


def solution(mesh):
    return jax.shard_map(
        per_device,
        mesh=mesh,
        in_specs=(
            P("head", ("grp", "row"), None, None),
            P("head", ("grp", "row"), None, "sub"),
            P("head", ("grp", "row"), None, "sub"),
            P("head", ("grp", "row"), None, None),
            P("head", ("grp", "row"), None, None),
            P("head", ("grp", "row"), None),
            P(("grp", "head"), "row", "sub"),
            P("grp"),
            P("grp", None),
        ),
        out_specs=(
            P("head", ("grp", "row"), None, "sub"),
            P("head", ("grp", "row"), None, "sub"),
            P("head", ("grp", "row"), None, "sub"),
            P(("grp", "head"), "row", "sub"),
        ),
        check_vma=False,
    )
```
